256 devices in a mesh: seq: 64 (over z, y_hi, x), head: 4 (over y_lo, core).
Axes of the slice: x: 4, y: 4 (y_hi: 2, y_lo: 2; y = y_hi * 2 + y_lo), z: 8, core: 2. Of those that a mesh axis runs over, the one named last changes fastest.
Arguments:
- queries: bfloat16 [32768, 4096], P('seq', 'head'), may hold values from -4.5 to 4.5
- key_heads: bfloat16 [32768, 1024], P('seq', 'head'), may hold values from -4.5 to 4.5
- value_head_rows: bfloat16 [32768, 1024], P('seq', 'head'), may hold values from -6 to 6
- out_grad: bfloat16 [32768, 4096], P('seq', 'head'), may hold values from -6 to 6
- doc_ids: int32 [32768], P('seq'), may hold values from 0 to 63, never falling along the last dimension, each value on 1 to 2048 neighbouring positions
Outputs:
- query_grad: bfloat16 [32768, 4096], P(('seq', 'head'))
- key_grad: bfloat16 [32768, 1024], P('seq', 'head')
- value_grad: bfloat16 [32768, 1024], P('seq', 'head')
The draws below stay inside these ranges and needn't reach their ends.
Inputs may be any that keep to these rules, and one draw needn't show every extreme that they name: `doc_ids`: never falling along the sequence; each document is 1 to 2048 tokens long and one is exactly 2048.
All inputs are finite; a program needn't handle non-finite values.
Results may differ from the reference program's by a relative error of at most 0.0072.
Values may be sent and summed in bfloat16 or wider, within the bound.
A program may use at most 128 MiB of HBM per device.

```python
import math
import jax
import jax.numpy as jnp
import numpy as np
from jax import lax

QUERY_HEADS = 32
KEY_VALUE_HEADS = 8
HEAD_SIZE = 128
TOK_DEV = 512
PACKED_TOKENS = 32768
WINDOW = 512
DOCS = 64
DOC_MOST = 2048
N_SEQ = 64


def draw_queries(key, part):
    key = jax.random.fold_in(key, 11)
    base_offset = jax.random.truncated_normal(key, -4.5, 4.5, (PACKED_TOKENS, QUERY_HEADS, HEAD_SIZE), jnp.float32)
    return base_offset.reshape(PACKED_TOKENS, QUERY_HEADS * HEAD_SIZE).astype(jnp.bfloat16)


def draw_key_heads(key, part):
    key = jax.random.fold_in(key, 12)
    base_offset = jax.random.truncated_normal(key, -4.5, 4.5, (PACKED_TOKENS, KEY_VALUE_HEADS, HEAD_SIZE), jnp.float32)
    return base_offset.reshape(PACKED_TOKENS, KEY_VALUE_HEADS * HEAD_SIZE).astype(jnp.bfloat16)


def level_of(stream_key, extent, pieces, least, high):
    factor_of, own = 1.0, jax.random.fold_in(stream_key, 6)
    for dim, parts in pieces:
        steps = jnp.exp(jax.random.uniform(jax.random.fold_in(own, dim), (parts,), jnp.float32, least / len(pieces), high / len(pieces)))
        factor_of = factor_of * jnp.repeat(steps, extent[dim] // parts).reshape([-1 if axis == dim else 1 for axis in range(len(extent))])
    return factor_of


def profile(amount, total, limit, lean):
    weights = [(1 << 20) // math.isqrt(standing ** lean) + 1 for standing in range(2, amount + 1)]
    surplus, holding = total - limit - (amount - 1), [1] * (amount - 1)
    while surplus > 0:
        free = [i for i in range(amount - 1) if holding[i] < limit]
        mass, remaining = sum([weights[i] for i in free]), surplus
        for i in free:
            addition = min(limit - holding[i], max(1, remaining * weights[i] // mass), surplus)
            holding[i] = holding[i] + addition
            surplus = surplus - addition
    return np.array([limit] + holding)


def uneven_parts(key, number_of, total, most, lean):
    if number_of == 2:
        one = jax.random.randint(key, (), max(1, total - most), min(most, total - 1) + 1)
        return jnp.stack([one, total - one])
    tallies = jnp.asarray(profile(number_of, total, most, lean), jnp.int32)
    pairs = (number_of - 1) // 2
    source_of, sink = tallies[1:1 + 2 * pairs:2], tallies[2:2 + 2 * pairs:2]
    room = jnp.minimum(source_of - 1, most - sink)
    moved = jax.random.randint(jax.random.fold_in(key, 1), (pairs,), 0, 1 << 20) % (room + 1)
    tallies = tallies.at[1:1 + 2 * pairs:2].set(source_of - moved).at[2:2 + 2 * pairs:2].set(sink + moved)
    return tallies[jax.random.permutation(jax.random.fold_in(key, 2), number_of)]


def centred(stream_key, shape, scale, reach, shards=(), kind=jnp.bfloat16):
    values = jax.random.normal(stream_key, shape, jnp.float32) * scale
    if len(shards) > 0:
        values = level_of(stream_key, shape, shards, -0.22, 0.18) * values
    return jnp.clip(values, min=-reach, max=reach).astype(kind)


def setup_inputs(seed: int = 0) -> dict:
    key_of = jax.random.split(jax.random.key(seed), 6)
    return {
        "queries": draw_queries(jax.random.fold_in(key_of[5], 71), 0),
        "key_heads": draw_key_heads(jax.random.fold_in(key_of[5], 71), 0),
        "value_head_rows": centred(key_of[2], (PACKED_TOKENS, KEY_VALUE_HEADS * HEAD_SIZE), 1.0, 6.0, ((0, 64), (1, 4))),
        "out_grad": centred(key_of[3], (PACKED_TOKENS, QUERY_HEADS * HEAD_SIZE), 1.0, 6.0, ((0, 64), (1, 4))),
        "doc_ids": jnp.searchsorted(jnp.cumsum(uneven_parts(key_of[4], DOCS, PACKED_TOKENS, DOC_MOST, 1)), jnp.arange(PACKED_TOKENS), side="right").astype(jnp.int32),
    }


masked_fill = -1e30


def block_grads(query_tile, gradient_block, key_tile, value_tile, keep_mask):
    row_number = query_tile.shape[0]
    key_number = key_tile.shape[0]
    score_scale = 1.0 / (HEAD_SIZE ** 0.5)
    query_pieces = query_tile.astype(jnp.float32).reshape(row_number, KEY_VALUE_HEADS, QUERY_HEADS // KEY_VALUE_HEADS, HEAD_SIZE)
    gradient_pieces = gradient_block.astype(jnp.float32).reshape(row_number, KEY_VALUE_HEADS, QUERY_HEADS // KEY_VALUE_HEADS, HEAD_SIZE)
    key_pieces = key_tile.astype(jnp.float32).reshape(key_number, KEY_VALUE_HEADS, HEAD_SIZE)
    value_pieces = value_tile.astype(jnp.float32).reshape(key_number, KEY_VALUE_HEADS, HEAD_SIZE)
    scores = jnp.einsum("rhgd,khd->hgrk", query_pieces, key_pieces) * score_scale
    scores = jnp.where(keep_mask, scores, masked_fill)
    row_top = jnp.max(scores, axis=-1, keepdims=True)
    row_sum = jnp.sum(jnp.where(keep_mask, jnp.exp(scores - row_top), 0.0), axis=-1, keepdims=True)
    log_total = row_top + jnp.log(row_sum)
    probs_full = jnp.where(keep_mask, jnp.exp(scores - log_total), 0.0)
    grad_probs = jnp.einsum("rhgd,khd->hgrk", gradient_pieces, value_pieces)
    delta_rows = jnp.sum(probs_full * grad_probs, axis=-1, keepdims=True)
    grad_scores = (probs_full * (grad_probs - delta_rows)).astype(jnp.bfloat16)
    grad_scores = lax.optimization_barrier(grad_scores).astype(jnp.float32)
    probs_round = lax.optimization_barrier(probs_full.astype(jnp.bfloat16)).astype(jnp.float32)
    query_portion = jnp.einsum("hgrk,khd->rhgd", grad_scores, key_pieces) * score_scale
    key_portion = jnp.einsum("hgrk,rhgd->khd", grad_scores, query_pieces) * score_scale
    value_portion = jnp.einsum("hgrk,rhgd->khd", probs_round, gradient_pieces)
    return (query_portion.reshape(row_number, QUERY_HEADS * HEAD_SIZE), key_portion.reshape(key_number, KEY_VALUE_HEADS * HEAD_SIZE),
            value_portion.reshape(key_number, KEY_VALUE_HEADS * HEAD_SIZE))


def reference(queries, key_heads, value_head_rows, out_grad, doc_ids):
    row_number = TOK_DEV
    positions = jnp.arange(row_number, dtype=jnp.int32)
    key_offsets = jnp.arange(2 * row_number, dtype=jnp.int32)

    def take_rows(array, start):
        return lax.dynamic_slice_in_dim(array, start, row_number, 0)

    def per_block(block):
        start = (block * row_number).astype(jnp.int32)
        prev_start = jnp.maximum(start - row_number, 0).astype(jnp.int32)
        query_tile = take_rows(queries, start)
        gradient_block = take_rows(out_grad, start)
        key_tile = jnp.concatenate([take_rows(key_heads, prev_start), take_rows(key_heads, start)], 0)
        value_tile = jnp.concatenate([take_rows(value_head_rows, prev_start), take_rows(value_head_rows, start)], 0)
        query_doc = take_rows(doc_ids, start)
        key_doc = jnp.concatenate([take_rows(doc_ids, prev_start), query_doc], 0)
        query_pos = start + positions
        key_pos = start - row_number + key_offsets
        keep_mask = ((key_pos[None, :] <= query_pos[:, None])
                     & (query_pos[:, None] - key_pos[None, :] < WINDOW)
                     & (key_pos[None, :] >= 0)
                     & (query_doc[:, None] == key_doc[None, :]))
        query_portion, key_portion, value_portion = block_grads(query_tile, gradient_block, key_tile, value_tile, keep_mask)
        return (query_portion.astype(jnp.bfloat16), key_portion[:row_number], key_portion[row_number:],
                value_portion[:row_number], value_portion[row_number:])

    results = lax.map(per_block, jnp.arange(N_SEQ, dtype=jnp.int32))
    query_grad = results[0].reshape(PACKED_TOKENS, QUERY_HEADS * HEAD_SIZE)

    def combine(cross_terms, local_terms):
        shifted_rows = jnp.concatenate([cross_terms[1:], jnp.zeros_like(cross_terms[:1])], 0)
        return (local_terms + shifted_rows).reshape(PACKED_TOKENS, KEY_VALUE_HEADS * HEAD_SIZE).astype(jnp.bfloat16)

    return query_grad, combine(results[1], results[2]), combine(results[3], results[4])
```

```python
import functools
import math

import jax
import jax.numpy as jnp
from jax import lax
from jax.experimental import pallas as pl
from jax.experimental.pallas import tpu as pltpu
from jax.sharding import PartitionSpec as P

HEAD = 128
TILE = 128
GROUPS = 2
SHARE = 4
BLOCK = 512
TILES = BLOCK // TILE
SPAN = BLOCK + TILE
WIDE = SHARE * HEAD
MASKED = -1e30
SCALE = 1.0 / math.sqrt(HEAD)
SCALE_LOG2 = SCALE * math.log2(math.e)
MESH = pl.DeviceIdType.MESH

NT = (((1,), (1,)), ((), ()))
NN = (((1,), (0,)), ((), ()))


def dot(a, b, dims):
    return lax.dot_general(a, b, dims, preferred_element_type=jnp.float32)


def kernel(
    n_seq,
    q_hbm, k_hbm, v_hbm, o_hbm, doc_hbm,
    dq_ref, dk_ref, dv_ref,
    q_s, o_s, k_s, v_s, kt_s, doc_s, docp_s, kdoc_s, bias_s, prob_s,
    dv_acc, dk_acc, back_s, back_r, dq_s,
    load_sem, kv_send, kv_recv, doc_send, doc_recv, dq_send, dq_recv, dq_own, back_send, back_recv,
):
    s = lax.axis_index("seq")
    h = lax.axis_index("head")
    following = (lax.rem(s + 1, n_seq), h)
    previous = (lax.rem(s + n_seq - 1, n_seq), h)

    loads = []

    def load(src, dst):
        copy = pltpu.make_async_copy(src, dst, load_sem.at[len(loads)])
        copy.start()
        loads.append(copy)

    load(doc_hbm, doc_s)
    for g in range(GROUPS):
        load(k_hbm.at[:, pl.ds(g * HEAD, HEAD)], k_s.at[g, pl.ds(BLOCK, BLOCK)])
        load(v_hbm.at[:, pl.ds(g * HEAD, HEAD)], v_s.at[g, pl.ds(BLOCK, BLOCK)])
    for r in range(GROUPS * SHARE):
        load(q_hbm.at[:, pl.ds(r * HEAD, HEAD)], q_s.at[r])
        load(o_hbm.at[:, pl.ds(r * HEAD, HEAD)], o_s.at[r])

    barrier = pltpu.get_barrier_semaphore()
    for peer in [following, previous] + [(s, lax.rem(h + d, 4)) for d in (1, 2, 3)]:
        pl.semaphore_signal(barrier, inc=1, device_id=peer, device_id_type=MESH)
    for copy in loads[: 1 + 2 * GROUPS]:
        copy.wait()
    pl.semaphore_wait(barrier, 5)

    doc_copy = pltpu.make_async_remote_copy(
        src_ref=doc_s, dst_ref=docp_s, send_sem=doc_send, recv_sem=doc_recv,
        device_id=following, device_id_type=MESH,
    )
    doc_copy.start()

    def kv_copy(buffer, which, g, i):
        slot = (g * 2 + which) * TILES + i
        return pltpu.make_async_remote_copy(
            src_ref=buffer.at[g, pl.ds(pl.multiple_of(BLOCK + i * TILE, TILE), TILE)],
            dst_ref=buffer.at[g, pl.ds(pl.multiple_of(i * TILE, TILE), TILE)],
            send_sem=kv_send.at[slot], recv_sem=kv_recv.at[slot],
            device_id=following, device_id_type=MESH,
        )

    for g in range(GROUPS):
        for which, buffer in ((0, k_s), (1, v_s)):
            for i in reversed(range(TILES)):
                kv_copy(buffer, which, g, i).start()

    for g in range(GROUPS):
        for j in range(TILES):
            rows = pl.ds(BLOCK + j * TILE, TILE)
            kt_s[g, :, rows] = k_s[g, rows, :].T
    dv_acc[...] = jnp.zeros_like(dv_acc)
    dk_acc[...] = jnp.zeros_like(dk_acc)

    doc_copy.wait()
    doc_own = doc_s[...].astype(jnp.float32)
    doc_prev = jnp.where(s > 0, docp_s[...].astype(jnp.float32), -1.0)
    for j in range(2 * TILES):
        source = doc_prev if j < TILES else doc_own
        row = source[j % TILES : j % TILES + 1, :]
        kdoc_s[j] = jnp.broadcast_to(row, (TILE, TILE)).T
    key_at = lax.broadcasted_iota(jnp.int32, (TILE, TILE), 0)
    query_at = lax.broadcasted_iota(jnp.int32, (TILE, TILE), 1)
    for i in range(TILES):
        query_doc = doc_own[i : i + 1, :]
        for j in range(TILES + 1):
            keep = kdoc_s[i + j] == query_doc
            if j == 0:
                keep = keep & (key_at > query_at)
            if j == TILES:
                keep = keep & (key_at <= query_at)
            bias_s[i, pl.ds(j * TILE, TILE), :] = jnp.where(keep, 0.0, MASKED)
    for copy in loads[1 + 2 * GROUPS :]:
        copy.wait()

    def back_copy(slot):
        return pltpu.make_async_remote_copy(
            src_ref=back_s.at[slot], dst_ref=back_r.at[slot],
            send_sem=back_send.at[slot], recv_sem=back_recv.at[slot],
            device_id=previous, device_id_type=MESH,
        )

    def dq_columns(owner, g):
        return pl.ds(pl.multiple_of(owner * (GROUPS * WIDE) + g * WIDE, WIDE), WIDE)

    def dq_copy(g, i):
        return pltpu.make_async_remote_copy(
            src_ref=dq_s.at[g * TILES + i], dst_ref=dq_ref.at[:, dq_columns(h, g)],
            send_sem=dq_send.at[g * TILES + i], recv_sem=dq_recv.at[g * TILES + h],
            device_id=(s, i), device_id_type=MESH,
        )

    def dq_local(g):
        return pltpu.make_async_copy(
            dq_s.at[g * TILES + h], dq_ref.at[:, dq_columns(h, g)], dq_own.at[g]
        )

    for g in range(GROUPS):
        def forward(step, carry, g=g):
            i = TILES - 1 - step
            kv_copy(k_s, 0, g, i).wait()
            rows = pl.ds(pl.multiple_of(i * TILE, TILE), TILE)
            span = pl.ds(pl.multiple_of(i * TILE, TILE), SPAN)
            kt_s[g, :, rows] = k_s[g, rows, :].T
            keys = k_s[g, span, :]
            bias = bias_s[i]
            rounded, outs = [], []
            for r in range(SHARE):
                scores = dot(keys, q_s[g * SHARE + r, rows, :], NT) * SCALE_LOG2 + bias
                top = jnp.max(scores, axis=0, keepdims=True)
                grown = jnp.exp2(scores - top)
                probs = grown * (1.0 / jnp.sum(grown, axis=0, keepdims=True))
                prob_s[i, :, pl.ds(r * HEAD, HEAD)] = probs
                rounded.append(probs.astype(jnp.bfloat16))
                outs.append(o_s[g * SHARE + r, rows, :])
            dv_acc[g, span, :] += dot(
                jnp.concatenate(rounded, axis=1), jnp.concatenate(outs, axis=0), NN
            )
            return carry

        lax.fori_loop(0, TILES, forward, 0)
        back_s[2 * g] = dv_acc[g, pl.ds(0, BLOCK), :].astype(jnp.bfloat16)
        back_copy(2 * g).start()

        def backward(step, carry, g=g):
            i = TILES - 1 - step
            kv_copy(v_s, 1, g, i).wait()
            rows = pl.ds(pl.multiple_of(i * TILE, TILE), TILE)
            span = pl.ds(pl.multiple_of(i * TILE, TILE), SPAN)
            values = v_s[g, span, :]
            rounded, queries = [], []
            for r in range(SHARE):
                grad_probs = dot(values, o_s[g * SHARE + r, rows, :], NT)
                probs = prob_s[i, :, pl.ds(r * HEAD, HEAD)]
                delta = jnp.sum(probs * grad_probs, axis=0, keepdims=True)
                rounded.append((probs * (grad_probs - delta)).astype(jnp.bfloat16))
                queries.append(q_s[g * SHARE + r, rows, :])
            grad_scores = jnp.concatenate(rounded, axis=1)
            dk_acc[g, span, :] += dot(grad_scores, jnp.concatenate(queries, axis=0), NN)
            dq_t = dot(kt_s[g, :, span], grad_scores, NN) * SCALE
            slot = g * TILES + i
            for r in range(SHARE):
                dq_s[slot, :, pl.ds(r * HEAD, HEAD)] = (
                    dq_t[:, r * HEAD : (r + 1) * HEAD].T.astype(jnp.bfloat16)
                )

            @pl.when(i != h)
            def _():
                dq_copy(g, i).start()

            @pl.when(i == h)
            def _():
                dq_local(g).start()

            return carry

        lax.fori_loop(0, TILES, backward, 0)
        back_s[2 * g + 1] = (dk_acc[g, pl.ds(0, BLOCK), :] * SCALE).astype(jnp.bfloat16)
        back_copy(2 * g + 1).start()

    for g in range(GROUPS):
        columns = pl.ds(g * HEAD, HEAD)
        back_copy(2 * g).wait()
        dv_ref[:, columns] = (
            dv_acc[g, pl.ds(BLOCK, BLOCK), :] + back_r[2 * g].astype(jnp.float32)
        ).astype(jnp.bfloat16)
        back_copy(2 * g + 1).wait()
        dk_ref[:, columns] = (
            dk_acc[g, pl.ds(BLOCK, BLOCK), :] * SCALE + back_r[2 * g + 1].astype(jnp.float32)
        ).astype(jnp.bfloat16)

    for g in range(GROUPS):
        dq_local(g).wait()
        for i in range(TILES):
            @pl.when(i != h)
            def _(g=g, i=i):
                dq_copy(g, i).wait_send()

        for d in (1, 2, 3):
            owner = lax.rem(h + d, 4)
            pltpu.make_async_remote_copy(
                src_ref=dq_s.at[g * TILES], dst_ref=dq_ref.at[:, dq_columns(owner, g)],
                send_sem=dq_send.at[g * TILES], recv_sem=dq_recv.at[g * TILES + owner],
                device_id=(s, owner), device_id_type=MESH,
            ).wait_recv()


def local(n_seq, queries, key_heads, value_head_rows, out_grad, doc_ids):
    bf16, f32 = jnp.bfloat16, jnp.float32
    dma = pltpu.SemaphoreType.DMA
    anywhere = pl.BlockSpec(memory_space=pl.ANY)
    vmem = pl.BlockSpec(memory_space=pltpu.VMEM)
    return pl.pallas_call(
        functools.partial(kernel, n_seq),
        out_shape=(
            jax.ShapeDtypeStruct((TILE, 4 * GROUPS * WIDE), bf16),
            jax.ShapeDtypeStruct((BLOCK, GROUPS * HEAD), bf16),
            jax.ShapeDtypeStruct((BLOCK, GROUPS * HEAD), bf16),
        ),
        in_specs=[anywhere] * 5,
        out_specs=(vmem, vmem, vmem),
        scratch_shapes=[
            pltpu.VMEM((GROUPS * SHARE, BLOCK, HEAD), bf16),
            pltpu.VMEM((GROUPS * SHARE, BLOCK, HEAD), bf16),
            pltpu.VMEM((GROUPS, 2 * BLOCK, HEAD), bf16),
            pltpu.VMEM((GROUPS, 2 * BLOCK, HEAD), bf16),
            pltpu.VMEM((GROUPS, HEAD, 2 * BLOCK), bf16),
            pltpu.VMEM((TILES, TILE), jnp.int32),
            pltpu.VMEM((TILES, TILE), jnp.int32),
            pltpu.VMEM((2 * TILES, TILE, TILE), f32),
            pltpu.VMEM((TILES, SPAN, TILE), f32),
            pltpu.VMEM((TILES, SPAN, WIDE), f32),
            pltpu.VMEM((GROUPS, 2 * BLOCK, HEAD), f32),
            pltpu.VMEM((GROUPS, 2 * BLOCK, HEAD), f32),
            pltpu.VMEM((2 * GROUPS, BLOCK, HEAD), bf16),
            pltpu.VMEM((2 * GROUPS, BLOCK, HEAD), bf16),
            pltpu.VMEM((GROUPS * TILES, TILE, WIDE), bf16),
            dma((1 + 2 * GROUPS + 2 * GROUPS * SHARE,)),
            dma((2 * GROUPS * TILES,)),
            dma((2 * GROUPS * TILES,)),
            dma(()),
            dma(()),
            dma((GROUPS * TILES,)),
            dma((GROUPS * TILES,)),
            dma((GROUPS,)),
            dma((2 * GROUPS,)),
            dma((2 * GROUPS,)),
        ],
        compiler_params=pltpu.CompilerParams(
            collective_id=0, has_side_effects=True, vmem_limit_bytes=48 * 2**20
        ),
    )(*[pltpu.with_memory_space_constraint(a, pltpu.HBM) for a in (queries, key_heads, value_head_rows, out_grad, doc_ids.reshape(TILES, TILE))])


def solution(mesh):
    placed = (P("seq", "head"), P("seq", "head"), P("seq", "head"), P("seq", "head"), P("seq"))
    return jax.shard_map(
        functools.partial(local, mesh.shape["seq"]),
        mesh=mesh,
        in_specs=placed,
        out_specs=(P(("seq", "head"), None), P("seq", "head"), P("seq", "head")),
        check_vma=False,
    )
```

```python
import functools
import math

import jax
import jax.numpy as jnp
from jax import lax
from jax.experimental import pallas as pl
from jax.experimental.pallas import tpu as pltpu
from jax.sharding import PartitionSpec as P

HEAD = 128
TILE = 128
GROUPS = 2
SHARE = 4
BLOCK = 512
TILES = BLOCK // TILE
SPAN = BLOCK + TILE
WIDE = SHARE * HEAD
PAIR = 2
MASKED = -1e30
SCALE = 1.0 / math.sqrt(HEAD)
SCALE_LOG2 = SCALE * math.log2(math.e)
MESH = pl.DeviceIdType.MESH

NT = (((1,), (1,)), ((), ()))
NN = (((1,), (0,)), ((), ()))
TN = (((0,), (0,)), ((), ()))


def dot(a, b, dims):
    return lax.dot_general(a, b, dims, preferred_element_type=jnp.float32)


def kernel(
    n_seq,
    q_hbm, k_hbm, v_hbm, o_hbm, doc_hbm,
    dq_ref, dk_ref, dv_ref,
    q_s, o_s, k_s, v_s, doc_s, docp_s, kdoc_s, bias_s, prob_s,
    dv_acc, dk_acc, back_s, back_r, dq_s,
    load_sem, kv_send, kv_recv, doc_send, doc_recv, dq_send, dq_recv, dq_own, back_send, back_recv,
):
    s = lax.axis_index("seq")
    h = lax.axis_index("head")
    following = (lax.rem(s + 1, n_seq), h)
    previous = (lax.rem(s + n_seq - 1, n_seq), h)

    loads = []

    def load(src, dst):
        copy = pltpu.make_async_copy(src, dst, load_sem.at[len(loads)])
        copy.start()
        loads.append(copy)

    load(doc_hbm, doc_s)
    for g in range(GROUPS):
        load(k_hbm.at[:, pl.ds(g * HEAD, HEAD)], k_s.at[g, pl.ds(BLOCK, BLOCK)])
        load(v_hbm.at[:, pl.ds(g * HEAD, HEAD)], v_s.at[g, pl.ds(BLOCK, BLOCK)])
    for r in range(GROUPS * SHARE):
        load(q_hbm.at[:, pl.ds(r * HEAD, HEAD)], q_s.at[r])
        load(o_hbm.at[:, pl.ds(r * HEAD, HEAD)], o_s.at[r])

    barrier = pltpu.get_barrier_semaphore()
    for peer in [following, previous] + [(s, lax.rem(h + d, 4)) for d in (1, 2, 3)]:
        pl.semaphore_signal(barrier, inc=1, device_id=peer, device_id_type=MESH)
    for copy in loads[: 1 + 2 * GROUPS]:
        copy.wait()
    pl.semaphore_wait(barrier, 5)

    doc_copy = pltpu.make_async_remote_copy(
        src_ref=doc_s, dst_ref=docp_s, send_sem=doc_send, recv_sem=doc_recv,
        device_id=following, device_id_type=MESH,
    )
    doc_copy.start()

    def kv_copy(buffer, which, g, i):
        slot = (g * 2 + which) * TILES + i
        return pltpu.make_async_remote_copy(
            src_ref=buffer.at[g, pl.ds(pl.multiple_of(BLOCK + i * TILE, TILE), TILE)],
            dst_ref=buffer.at[g, pl.ds(pl.multiple_of(i * TILE, TILE), TILE)],
            send_sem=kv_send.at[slot], recv_sem=kv_recv.at[slot],
            device_id=following, device_id_type=MESH,
        )

    for g in range(GROUPS):
        for which, buffer in ((0, k_s), (1, v_s)):
            for i in reversed(range(TILES)):
                kv_copy(buffer, which, g, i).start()

    dv_acc[...] = jnp.zeros_like(dv_acc)
    dk_acc[...] = jnp.zeros_like(dk_acc)

    doc_copy.wait()
    doc_own = doc_s[...].astype(jnp.float32)
    doc_prev = jnp.where(s > 0, docp_s[...].astype(jnp.float32), -1.0)
    for j in range(2 * TILES):
        source = doc_prev if j < TILES else doc_own
        row = source[j % TILES : j % TILES + 1, :]
        kdoc_s[j] = jnp.broadcast_to(row, (TILE, TILE)).T
    key_at = lax.broadcasted_iota(jnp.int32, (TILE, TILE), 0)
    query_at = lax.broadcasted_iota(jnp.int32, (TILE, TILE), 1)
    for i in range(TILES):
        query_doc = doc_own[i : i + 1, :]
        for j in range(TILES + 1):
            keep = kdoc_s[i + j] == query_doc
            if j == 0:
                keep = keep & (key_at > query_at)
            if j == TILES:
                keep = keep & (key_at <= query_at)
            bias_s[i, pl.ds(j * TILE, TILE), :] = jnp.where(keep, 0.0, MASKED)
    for copy in loads[1 + 2 * GROUPS :]:
        copy.wait()

    def back_copy(slot):
        return pltpu.make_async_remote_copy(
            src_ref=back_s.at[slot], dst_ref=back_r.at[slot],
            send_sem=back_send.at[slot], recv_sem=back_recv.at[slot],
            device_id=previous, device_id_type=MESH,
        )

    def dq_columns(owner, g):
        return pl.ds(pl.multiple_of(owner * (GROUPS * WIDE) + g * WIDE, WIDE), WIDE)

    def dq_copy(g, i):
        return pltpu.make_async_remote_copy(
            src_ref=dq_s.at[g * TILES + i], dst_ref=dq_ref.at[:, dq_columns(h, g)],
            send_sem=dq_send.at[g * TILES + i], recv_sem=dq_recv.at[g * TILES + h],
            device_id=(s, i), device_id_type=MESH,
        )

    def dq_local(g):
        return pltpu.make_async_copy(
            dq_s.at[g * TILES + h], dq_ref.at[:, dq_columns(h, g)], dq_own.at[g]
        )

    for g in range(GROUPS):
        def forward(step, carry, g=g):
            i = TILES - 1 - step
            kv_copy(k_s, 0, g, i).wait()
            rows = pl.ds(pl.multiple_of(i * TILE, TILE), TILE)
            span = pl.ds(pl.multiple_of(i * TILE, TILE), SPAN)
            keys = k_s[g, span, :]
            bias = bias_s[i]
            outs = [o_s[g * SHARE + r, rows, :] for r in range(SHARE)]
            rounded = []
            for r in range(0, SHARE, PAIR):
                queries = [q_s[g * SHARE + e, rows, :] for e in range(r, r + PAIR)]
                joined = dot(keys, jnp.concatenate(queries, axis=0), NT)
                for e in range(PAIR):
                    scores = joined[:, e * HEAD : (e + 1) * HEAD] * SCALE_LOG2 + bias
                    top = jnp.max(scores, axis=0, keepdims=True)
                    grown = jnp.exp2(scores - top)
                    probs = grown * (1.0 / jnp.sum(grown, axis=0, keepdims=True))
                    prob_s[i, :, pl.ds((r + e) * HEAD, HEAD)] = probs
                    rounded.append(probs.astype(jnp.bfloat16))
            dv_acc[g, span, :] += dot(
                jnp.concatenate(rounded, axis=1), jnp.concatenate(outs, axis=0), NN
            )
            return carry

        lax.fori_loop(0, TILES, forward, 0)
        back_s[2 * g] = dv_acc[g, pl.ds(0, BLOCK), :].astype(jnp.bfloat16)
        back_copy(2 * g).start()

        def backward(step, carry, g=g):
            i = TILES - 1 - step
            kv_copy(v_s, 1, g, i).wait()
            rows = pl.ds(pl.multiple_of(i * TILE, TILE), TILE)
            span = pl.ds(pl.multiple_of(i * TILE, TILE), SPAN)
            values = v_s[g, span, :]
            queries = [q_s[g * SHARE + r, rows, :] for r in range(SHARE)]
            rounded = []
            for r in range(0, SHARE, PAIR):
                outs = [o_s[g * SHARE + e, rows, :] for e in range(r, r + PAIR)]
                joined = dot(values, jnp.concatenate(outs, axis=0), NT)
                for e in range(PAIR):
                    grad_probs = joined[:, e * HEAD : (e + 1) * HEAD]
                    probs = prob_s[i, :, pl.ds((r + e) * HEAD, HEAD)]
                    delta = jnp.sum(probs * grad_probs, axis=0, keepdims=True)
                    rounded.append((probs * (grad_probs - delta)).astype(jnp.bfloat16))
            grad_scores = jnp.concatenate(rounded, axis=1)
            dk_acc[g, span, :] += dot(grad_scores, jnp.concatenate(queries, axis=0), NN)
            slot = g * TILES + i
            grads = dot(grad_scores, k_s[g, span, :], TN) * SCALE
            for r in range(SHARE):
                dq_s[slot, :, pl.ds(r * HEAD, HEAD)] = (
                    grads[r * HEAD : (r + 1) * HEAD, :].astype(jnp.bfloat16)
                )

            @pl.when(i != h)
            def _():
                dq_copy(g, i).start()

            @pl.when(i == h)
            def _():
                dq_local(g).start()

            return carry

        lax.fori_loop(0, TILES, backward, 0)
        back_s[2 * g + 1] = (dk_acc[g, pl.ds(0, BLOCK), :] * SCALE).astype(jnp.bfloat16)
        back_copy(2 * g + 1).start()

    for g in range(GROUPS):
        columns = pl.ds(g * HEAD, HEAD)
        back_copy(2 * g).wait()
        dv_ref[:, columns] = (
            dv_acc[g, pl.ds(BLOCK, BLOCK), :] + back_r[2 * g].astype(jnp.float32)
        ).astype(jnp.bfloat16)
        back_copy(2 * g + 1).wait()
        dk_ref[:, columns] = (
            dk_acc[g, pl.ds(BLOCK, BLOCK), :] * SCALE + back_r[2 * g + 1].astype(jnp.float32)
        ).astype(jnp.bfloat16)

    for g in range(GROUPS):
        dq_local(g).wait()
        for i in range(TILES):
            @pl.when(i != h)
            def _(g=g, i=i):
                dq_copy(g, i).wait_send()

        for d in (1, 2, 3):
            owner = lax.rem(h + d, 4)
            pltpu.make_async_remote_copy(
                src_ref=dq_s.at[g * TILES], dst_ref=dq_ref.at[:, dq_columns(owner, g)],
                send_sem=dq_send.at[g * TILES], recv_sem=dq_recv.at[g * TILES + owner],
                device_id=(s, owner), device_id_type=MESH,
            ).wait_recv()


def write_out(a_ref, b_ref, c_ref, a_out, b_out, c_out, sem):
    copies = [
        pltpu.make_async_copy(src, dst, sem.at[slot])
        for slot, (src, dst) in enumerate(((a_ref, a_out), (b_ref, b_out), (c_ref, c_out)))
    ]
    for copy in copies:
        copy.start()
    for copy in copies:
        copy.wait()


def local(n_seq, queries, key_heads, value_head_rows, out_grad, doc_ids):
    bf16, f32 = jnp.bfloat16, jnp.float32
    dma = pltpu.SemaphoreType.DMA
    anywhere = pl.BlockSpec(memory_space=pl.ANY)
    vmem = pl.BlockSpec(memory_space=pltpu.VMEM)
    shapes = (
            jax.ShapeDtypeStruct((TILE, 4 * GROUPS * WIDE), bf16),
            jax.ShapeDtypeStruct((BLOCK, GROUPS * HEAD), bf16),
            jax.ShapeDtypeStruct((BLOCK, GROUPS * HEAD), bf16),
    )
    grads = pl.pallas_call(
        functools.partial(kernel, n_seq),
        out_shape=shapes,
        in_specs=[anywhere] * 5,
        out_specs=(vmem, vmem, vmem),
        scratch_shapes=[
            pltpu.VMEM((GROUPS * SHARE, BLOCK, HEAD), bf16),
            pltpu.VMEM((GROUPS * SHARE, BLOCK, HEAD), bf16),
            pltpu.VMEM((GROUPS, 2 * BLOCK, HEAD), bf16),
            pltpu.VMEM((GROUPS, 2 * BLOCK, HEAD), bf16),
            pltpu.VMEM((TILES, TILE), jnp.int32),
            pltpu.VMEM((TILES, TILE), jnp.int32),
            pltpu.VMEM((2 * TILES, TILE, TILE), f32),
            pltpu.VMEM((TILES, SPAN, TILE), f32),
            pltpu.VMEM((TILES, SPAN, WIDE), f32),
            pltpu.VMEM((GROUPS, 2 * BLOCK, HEAD), f32),
            pltpu.VMEM((GROUPS, 2 * BLOCK, HEAD), f32),
            pltpu.VMEM((2 * GROUPS, BLOCK, HEAD), bf16),
            pltpu.VMEM((2 * GROUPS, BLOCK, HEAD), bf16),
            pltpu.VMEM((GROUPS * TILES, TILE, WIDE), bf16),
            dma((1 + 2 * GROUPS + 2 * GROUPS * SHARE,)),
            dma((2 * GROUPS * TILES,)),
            dma((2 * GROUPS * TILES,)),
            dma(()),
            dma(()),
            dma((GROUPS * TILES,)),
            dma((GROUPS * TILES,)),
            dma((GROUPS,)),
            dma((2 * GROUPS,)),
            dma((2 * GROUPS,)),
        ],
        compiler_params=pltpu.CompilerParams(
            collective_id=0, has_side_effects=True, vmem_limit_bytes=48 * 2**20
        ),
    )(*[pltpu.with_memory_space_constraint(a, pltpu.HBM) for a in (queries, key_heads, value_head_rows, out_grad, doc_ids.reshape(TILES, TILE))])

    return pl.pallas_call(
        write_out,
        out_shape=shapes,
        in_specs=[vmem] * 3,
        out_specs=(anywhere,) * 3,
        scratch_shapes=[dma((3,))],
    )(*[pltpu.with_memory_space_constraint(a, pltpu.VMEM) for a in grads])


def solution(mesh):
    placed = (P("seq", "head"), P("seq", "head"), P("seq", "head"), P("seq", "head"), P("seq"))
    return jax.shard_map(
        functools.partial(local, mesh.shape["seq"]),
        mesh=mesh,
        in_specs=placed,
        out_specs=(P(("seq", "head"), None), P("seq", "head"), P("seq", "head")),
        check_vma=False,
    )
```

```python
import functools
import math

import jax
import jax.numpy as jnp
from jax import lax
from jax.experimental import pallas as pl
from jax.experimental.pallas import tpu as pltpu
from jax.sharding import PartitionSpec as P

HEAD = 128
TILE = 128
GROUPS = 2
SHARE = 4
BLOCK = 512
TILES = BLOCK // TILE
SPAN = BLOCK + TILE
WIDE = SHARE * HEAD
PAIR = 2
LINE = 4
RELAYED = (2,)
PARTS = ((3, 2), (1, 0))
MASKED = -1e30
SCALE = 1.0 / math.sqrt(HEAD)
SCALE_LOG2 = SCALE * math.log2(math.e)
MESH = pl.DeviceIdType.MESH

NT = (((1,), (1,)), ((), ()))
NN = (((1,), (0,)), ((), ()))
TN = (((0,), (0,)), ((), ()))


def dot(a, b, dims):
    return lax.dot_general(a, b, dims, preferred_element_type=jnp.float32)


def kernel(
    n_seq,
    q_hbm, k_hbm, v_hbm, o_hbm, doc_hbm,
    dq_ref, dk_ref, dv_ref,
    q_s, o_s, k_s, v_s, doc_s, docp_s, kdoc_s, bias_s, prob_s, share_s, outs_s,
    dv_acc, dk_acc, back_s, back_r, relay_s, dq_s,
    load_sem, kv_send, kv_recv, doc_send, doc_recv, dq_send, dq_recv, dq_own, back_send, back_recv,
    relay_send, relay_recv,
):
    s = lax.axis_index("seq")
    h = lax.axis_index("head")
    following = (lax.rem(s + 1, n_seq), h)
    previous = (lax.rem(s + n_seq - 1, n_seq), h)
    place = lax.rem(s, LINE)
    first, third = place == 0, place == 2
    partner = (lax.rem(s + jnp.where(place < 2, n_seq - 2, 2), n_seq), h)

    loads = []

    def load(src, dst):
        copy = pltpu.make_async_copy(src, dst, load_sem.at[len(loads)])
        copy.start()
        loads.append(copy)

    load(doc_hbm, doc_s)
    for g in range(GROUPS):
        load(k_hbm.at[:, pl.ds(g * HEAD, HEAD)], k_s.at[g, pl.ds(BLOCK, BLOCK)])
        load(v_hbm.at[:, pl.ds(g * HEAD, HEAD)], v_s.at[g, pl.ds(BLOCK, BLOCK)])
    for r in range(GROUPS * SHARE):
        load(q_hbm.at[:, pl.ds(r * HEAD, HEAD)], q_s.at[r])
        load(o_hbm.at[:, pl.ds(r * HEAD, HEAD)], o_s.at[r])

    barrier = pltpu.get_barrier_semaphore()
    for peer in [following, previous, partner] + [(s, lax.rem(h + d, 4)) for d in (1, 2, 3)]:
        pl.semaphore_signal(barrier, inc=1, device_id=peer, device_id_type=MESH)
    for copy in loads[: 1 + 2 * GROUPS]:
        copy.wait()
    pl.semaphore_wait(barrier, 6)

    doc_copy = pltpu.make_async_remote_copy(
        src_ref=doc_s, dst_ref=docp_s, send_sem=doc_send, recv_sem=doc_recv,
        device_id=following, device_id_type=MESH,
    )
    doc_copy.start()

    def kv_copy(buffer, which, g, i):
        slot = (g * 2 + which) * TILES + i
        return pltpu.make_async_remote_copy(
            src_ref=buffer.at[g, pl.ds(pl.multiple_of(BLOCK + i * TILE, TILE), TILE)],
            dst_ref=buffer.at[g, pl.ds(pl.multiple_of(i * TILE, TILE), TILE)],
            send_sem=kv_send.at[slot], recv_sem=kv_recv.at[slot],
            device_id=following, device_id_type=MESH,
        )

    for g in range(GROUPS):
        for which, buffer in ((0, k_s), (1, v_s)):
            for i in reversed(range(TILES)):
                kv_copy(buffer, which, g, i).start()

    dv_acc[...] = jnp.zeros_like(dv_acc)
    dk_acc[...] = jnp.zeros_like(dk_acc)

    doc_copy.wait()
    doc_own = doc_s[...].astype(jnp.float32)
    doc_prev = jnp.where(s > 0, docp_s[...].astype(jnp.float32), -1.0)
    for j in range(2 * TILES):
        source = doc_prev if j < TILES else doc_own
        row = source[j % TILES : j % TILES + 1, :]
        kdoc_s[j] = jnp.broadcast_to(row, (TILE, TILE)).T
    key_at = lax.broadcasted_iota(jnp.int32, (TILE, TILE), 0)
    query_at = lax.broadcasted_iota(jnp.int32, (TILE, TILE), 1)
    for i in range(TILES):
        query_doc = doc_own[i : i + 1, :]
        for j in range(TILES + 1):
            keep = kdoc_s[i + j] == query_doc
            if j == 0:
                keep = keep & (key_at > query_at)
            if j == TILES:
                keep = keep & (key_at <= query_at)
            bias_s[i, pl.ds(j * TILE, TILE), :] = jnp.where(keep, 0.0, MASKED)
    for copy in loads[1 + 2 * GROUPS :]:
        copy.wait()

    def back_copy(slot):
        return pltpu.make_async_remote_copy(
            src_ref=back_s.at[slot], dst_ref=back_r.at[slot],
            send_sem=back_send.at[slot], recv_sem=back_recv.at[slot],
            device_id=previous, device_id_type=MESH,
        )

    def relay_copy(slot):
        lane = RELAYED.index(slot)
        return pltpu.make_async_remote_copy(
            src_ref=back_s.at[slot], dst_ref=relay_s.at[lane],
            send_sem=back_send.at[slot], recv_sem=relay_recv.at[lane],
            device_id=partner, device_id_type=MESH,
        )

    def onward_copy(slot):
        lane = RELAYED.index(slot)
        return pltpu.make_async_remote_copy(
            src_ref=relay_s.at[lane], dst_ref=back_r.at[slot],
            send_sem=relay_send.at[lane], recv_sem=back_recv.at[slot],
            device_id=following, device_id_type=MESH,
        )

    def send_back(slot):
        if slot not in RELAYED:
            back_copy(slot).start()
            return

        @pl.when(first)
        def _():
            relay_copy(slot).start()

        @pl.when(jnp.logical_not(first))
        def _():
            back_copy(slot).start()

    def pass_on(slot):
        @pl.when(third)
        def _():
            relay_copy(slot).wait_recv()
            onward_copy(slot).start()

    def dq_columns(owner, g):
        return pl.ds(pl.multiple_of(owner * (GROUPS * WIDE) + g * WIDE, WIDE), WIDE)

    def dq_copy(g, i):
        return pltpu.make_async_remote_copy(
            src_ref=dq_s.at[g * TILES + i], dst_ref=dq_ref.at[:, dq_columns(h, g)],
            send_sem=dq_send.at[g * TILES + i], recv_sem=dq_recv.at[g * TILES + h],
            device_id=(s, i), device_id_type=MESH,
        )

    def dq_local(g):
        return pltpu.make_async_copy(
            dq_s.at[g * TILES + h], dq_ref.at[:, dq_columns(h, g)], dq_own.at[g]
        )

    def forward(g, i):
        rows, span = pl.ds(i * TILE, TILE), pl.ds(i * TILE, SPAN)
        keys = k_s[g, span, :]
        bias = bias_s[i]
        for r in range(0, SHARE, PAIR):
            queries = [q_s[g * SHARE + e, rows, :] for e in range(r, r + PAIR)]
            joined = dot(keys, jnp.concatenate(queries, axis=0), NT)
            for e in range(PAIR):
                scores = joined[:, e * HEAD : (e + 1) * HEAD] * SCALE_LOG2 + bias
                top = jnp.max(scores, axis=0, keepdims=True)
                grown = jnp.exp2(scores - top)
                share = 1.0 / jnp.sum(grown, axis=0, keepdims=True)
                prob_s[i, :, pl.ds((r + e) * HEAD, HEAD)] = grown.astype(jnp.bfloat16)
                share_s[i, pl.ds(r + e, 1), :] = share
                column = jnp.broadcast_to(share, (TILE, TILE)).T
                outs = o_s[g * SHARE + r + e, rows, :].astype(jnp.float32) * column
                outs_s[i, pl.ds((r + e) * TILE, TILE), :] = outs.astype(jnp.bfloat16)
        dv_acc[g, span, :] += dot(prob_s[i], outs_s[i], NN)

    def backward(g, i):
        rows, span = pl.ds(i * TILE, TILE), pl.ds(i * TILE, SPAN)
        values = v_s[g, span, :]
        queries = [q_s[g * SHARE + r, rows, :] for r in range(SHARE)]
        rounded = []
        for r in range(0, SHARE, PAIR):
            joined = dot(values, outs_s[i, pl.ds(r * TILE, PAIR * TILE), :], NT)
            for e in range(PAIR):
                grad_probs = joined[:, e * HEAD : (e + 1) * HEAD]
                grown = prob_s[i, :, pl.ds((r + e) * HEAD, HEAD)].astype(jnp.float32)
                delta = jnp.sum(grown * grad_probs, axis=0, keepdims=True)
                delta = delta * share_s[i, pl.ds(r + e, 1), :]
                rounded.append((grown * (grad_probs - delta)).astype(jnp.bfloat16))
        grad_scores = jnp.concatenate(rounded, axis=1)
        dk_acc[g, span, :] += dot(grad_scores, jnp.concatenate(queries, axis=0), NN)
        slot = g * TILES + i
        grads = dot(grad_scores, k_s[g, span, :], TN) * SCALE
        for r in range(SHARE):
            dq_s[slot, :, pl.ds(r * HEAD, HEAD)] = (
                grads[r * HEAD : (r + 1) * HEAD, :].astype(jnp.bfloat16)
            )


    def dq_start(g, i):
        @pl.when(i != h)
        def _():
            dq_copy(g, i).start()

        @pl.when(i == h)
        def _():
            dq_local(g).start()

    def forward_phase(g, parts):
        for part in parts:
            for i in part:
                kv_copy(k_s, 0, g, i).wait()
            for i in part:
                forward(g, i)
        back_s[2 * g] = dv_acc[g, pl.ds(0, BLOCK), :].astype(jnp.bfloat16)
        send_back(2 * g)

    def backward_phase(g, parts):
        for part in parts:
            for i in part:
                kv_copy(v_s, 1, g, i).wait()
            for i in part:
                backward(g, i)
            if part is parts[-1]:
                back_s[2 * g + 1] = (dk_acc[g, pl.ds(0, BLOCK), :] * SCALE).astype(jnp.bfloat16)
                send_back(2 * g + 1)
            for i in part:
                dq_start(g, i)

    for g in range(GROUPS):
        forward_phase(g, PARTS)
        backward_phase(g, PARTS)

    for slot in RELAYED:
        pass_on(slot)

    for g in range(GROUPS):
        columns = pl.ds(g * HEAD, HEAD)
        back_copy(2 * g).wait()
        dv_ref[:, columns] = (
            dv_acc[g, pl.ds(BLOCK, BLOCK), :] + back_r[2 * g].astype(jnp.float32)
        ).astype(jnp.bfloat16)
        back_copy(2 * g + 1).wait()
        dk_ref[:, columns] = (
            dk_acc[g, pl.ds(BLOCK, BLOCK), :] * SCALE + back_r[2 * g + 1].astype(jnp.float32)
        ).astype(jnp.bfloat16)

    for slot in RELAYED:
        @pl.when(third)
        def _(slot=slot):
            onward_copy(slot).wait_send()

    for g in range(GROUPS):
        dq_local(g).wait()
        for i in range(TILES):
            @pl.when(i != h)
            def _(g=g, i=i):
                dq_copy(g, i).wait_send()

        for d in (1, 2, 3):
            owner = lax.rem(h + d, 4)
            pltpu.make_async_remote_copy(
                src_ref=dq_s.at[g * TILES], dst_ref=dq_ref.at[:, dq_columns(owner, g)],
                send_sem=dq_send.at[g * TILES], recv_sem=dq_recv.at[g * TILES + owner],
                device_id=(s, owner), device_id_type=MESH,
            ).wait_recv()


def write_out(a_ref, b_ref, c_ref, a_out, b_out, c_out, sem):
    copies = [
        pltpu.make_async_copy(src, dst, sem.at[slot])
        for slot, (src, dst) in enumerate(((a_ref, a_out), (b_ref, b_out), (c_ref, c_out)))
    ]
    for copy in copies:
        copy.start()
    for copy in copies:
        copy.wait()


def local(n_seq, queries, key_heads, value_head_rows, out_grad, doc_ids):
    bf16, f32 = jnp.bfloat16, jnp.float32
    dma = pltpu.SemaphoreType.DMA
    anywhere = pl.BlockSpec(memory_space=pl.ANY)
    vmem = pl.BlockSpec(memory_space=pltpu.VMEM)
    shapes = (
            jax.ShapeDtypeStruct((TILE, 4 * GROUPS * WIDE), bf16),
            jax.ShapeDtypeStruct((BLOCK, GROUPS * HEAD), bf16),
            jax.ShapeDtypeStruct((BLOCK, GROUPS * HEAD), bf16),
    )
    grads = pl.pallas_call(
        functools.partial(kernel, n_seq),
        out_shape=shapes,
        in_specs=[anywhere] * 5,
        out_specs=(vmem, vmem, vmem),
        scratch_shapes=[
            pltpu.VMEM((GROUPS * SHARE, BLOCK, HEAD), bf16),
            pltpu.VMEM((GROUPS * SHARE, BLOCK, HEAD), bf16),
            pltpu.VMEM((GROUPS, 2 * BLOCK, HEAD), bf16),
            pltpu.VMEM((GROUPS, 2 * BLOCK, HEAD), bf16),
            pltpu.VMEM((TILES, TILE), jnp.int32),
            pltpu.VMEM((TILES, TILE), jnp.int32),
            pltpu.VMEM((2 * TILES, TILE, TILE), f32),
            pltpu.VMEM((TILES, SPAN, TILE), f32),
            pltpu.VMEM((TILES, SPAN, WIDE), bf16),
            pltpu.VMEM((TILES, 8, TILE), f32),
            pltpu.VMEM((TILES, SHARE * TILE, HEAD), bf16),
            pltpu.VMEM((GROUPS, 2 * BLOCK, HEAD), f32),
            pltpu.VMEM((GROUPS, 2 * BLOCK, HEAD), f32),
            pltpu.VMEM((2 * GROUPS, BLOCK, HEAD), bf16),
            pltpu.VMEM((2 * GROUPS, BLOCK, HEAD), bf16),
            pltpu.VMEM((len(RELAYED), BLOCK, HEAD), bf16),
            pltpu.VMEM((GROUPS * TILES, TILE, WIDE), bf16),
            dma((1 + 2 * GROUPS + 2 * GROUPS * SHARE,)),
            dma((2 * GROUPS * TILES,)),
            dma((2 * GROUPS * TILES,)),
            dma(()),
            dma(()),
            dma((GROUPS * TILES,)),
            dma((GROUPS * TILES,)),
            dma((GROUPS,)),
            dma((2 * GROUPS,)),
            dma((2 * GROUPS,)),
            dma((len(RELAYED),)),
            dma((len(RELAYED),)),
        ],
        compiler_params=pltpu.CompilerParams(
            collective_id=0, has_side_effects=True, vmem_limit_bytes=48 * 2**20
        ),
    )(*[pltpu.with_memory_space_constraint(a, pltpu.HBM) for a in (queries, key_heads, value_head_rows, out_grad, doc_ids.reshape(TILES, TILE))])

    return pl.pallas_call(
        write_out,
        out_shape=shapes,
        in_specs=[vmem] * 3,
        out_specs=(anywhere,) * 3,
        scratch_shapes=[dma((3,))],
    )(*[pltpu.with_memory_space_constraint(a, pltpu.VMEM) for a in grads])


def solution(mesh):
    placed = (P("seq", "head"), P("seq", "head"), P("seq", "head"), P("seq", "head"), P("seq"))
    return jax.shard_map(
        functools.partial(local, mesh.shape["seq"]),
        mesh=mesh,
        in_specs=placed,
        out_specs=(P(("seq", "head"), None), P("seq", "head"), P("seq", "head")),
        check_vma=False,
    )
```

```python
import functools
import math

import jax
import jax.numpy as jnp
from jax import lax
from jax.experimental import pallas as pl
from jax.experimental.pallas import tpu as pltpu
from jax.sharding import PartitionSpec as P

HEAD = 128
TILE = 128
GROUPS = 2
SHARE = 4
BLOCK = 512
TILES = BLOCK // TILE
SPAN = BLOCK + TILE
WIDE = SHARE * HEAD
PAIR = 1
LINE = 4
RELAYED = (2,)
PARTS = ((3, 2), (1, 0))
MASKED = -1e30
SCALE = 1.0 / math.sqrt(HEAD)
SCALE_LOG2 = SCALE * math.log2(math.e)
MESH = pl.DeviceIdType.MESH

NT = (((1,), (1,)), ((), ()))
NN = (((1,), (0,)), ((), ()))
TN = (((0,), (0,)), ((), ()))


def dot(a, b, dims):
    return lax.dot_general(a, b, dims, preferred_element_type=jnp.float32)


def kernel(
    n_seq,
    q_hbm, k_hbm, v_hbm, o_hbm, doc_hbm,
    dq_ref, dk_ref, dv_ref,
    q_s, o_s, k_s, v_s, doc_s, docp_s, kdoc_s, bias_s, prob_s, share_s, outs_s,
    dv_acc, dk_acc, back_s, back_r, relay_s, dq_s,
    load_sem, kv_send, kv_recv, doc_send, doc_recv, dq_send, dq_recv, dq_own, back_send, back_recv,
    relay_send, relay_recv,
):
    s = lax.axis_index("seq")
    h = lax.axis_index("head")
    following = (lax.rem(s + 1, n_seq), h)
    previous = (lax.rem(s + n_seq - 1, n_seq), h)
    place = lax.rem(s, LINE)
    first, third = place == 0, place == 2
    partner = (lax.rem(s + jnp.where(place < 2, n_seq - 2, 2), n_seq), h)

    loads = []

    def load(src, dst):
        copy = pltpu.make_async_copy(src, dst, load_sem.at[len(loads)])
        copy.start()
        loads.append(copy)

    load(doc_hbm, doc_s)
    for g in range(GROUPS):
        load(k_hbm.at[:, pl.ds(g * HEAD, HEAD)], k_s.at[g, pl.ds(BLOCK, BLOCK)])
        load(v_hbm.at[:, pl.ds(g * HEAD, HEAD)], v_s.at[g, pl.ds(BLOCK, BLOCK)])
    for r in range(GROUPS * SHARE):
        load(q_hbm.at[:, pl.ds(r * HEAD, HEAD)], q_s.at[r])
        load(o_hbm.at[:, pl.ds(r * HEAD, HEAD)], o_s.at[r])

    barrier = pltpu.get_barrier_semaphore()
    for peer in [following, previous, partner] + [(s, lax.rem(h + d, 4)) for d in (1, 2, 3)]:
        pl.semaphore_signal(barrier, inc=1, device_id=peer, device_id_type=MESH)
    for copy in loads[: 1 + 2 * GROUPS]:
        copy.wait()
    pl.semaphore_wait(barrier, 6)

    doc_copy = pltpu.make_async_remote_copy(
        src_ref=doc_s, dst_ref=docp_s, send_sem=doc_send, recv_sem=doc_recv,
        device_id=following, device_id_type=MESH,
    )
    doc_copy.start()

    def kv_copy(buffer, which, g, i):
        slot = (g * 2 + which) * TILES + i
        return pltpu.make_async_remote_copy(
            src_ref=buffer.at[g, pl.ds(pl.multiple_of(BLOCK + i * TILE, TILE), TILE)],
            dst_ref=buffer.at[g, pl.ds(pl.multiple_of(i * TILE, TILE), TILE)],
            send_sem=kv_send.at[slot], recv_sem=kv_recv.at[slot],
            device_id=following, device_id_type=MESH,
        )

    for g in range(GROUPS):
        for which, buffer in ((0, k_s), (1, v_s)):
            for i in reversed(range(TILES)):
                kv_copy(buffer, which, g, i).start()

    dv_acc[...] = jnp.zeros_like(dv_acc)
    dk_acc[...] = jnp.zeros_like(dk_acc)

    doc_copy.wait()
    doc_own = doc_s[...].astype(jnp.float32)
    doc_prev = jnp.where(s > 0, docp_s[...].astype(jnp.float32), -1.0)
    for j in range(2 * TILES):
        source = doc_prev if j < TILES else doc_own
        row = source[j % TILES : j % TILES + 1, :]
        kdoc_s[j] = jnp.broadcast_to(row, (TILE, TILE)).T
    key_at = lax.broadcasted_iota(jnp.int32, (TILE, TILE), 0)
    query_at = lax.broadcasted_iota(jnp.int32, (TILE, TILE), 1)
    for i in range(TILES):
        query_doc = doc_own[i : i + 1, :]
        for j in range(TILES + 1):
            keep = kdoc_s[i + j] == query_doc
            if j == 0:
                keep = keep & (key_at > query_at)
            if j == TILES:
                keep = keep & (key_at <= query_at)
            bias_s[i, pl.ds(j * TILE, TILE), :] = jnp.where(keep, 0.0, MASKED)
    for copy in loads[1 + 2 * GROUPS :]:
        copy.wait()

    def back_copy(slot):
        return pltpu.make_async_remote_copy(
            src_ref=back_s.at[slot], dst_ref=back_r.at[slot],
            send_sem=back_send.at[slot], recv_sem=back_recv.at[slot],
            device_id=previous, device_id_type=MESH,
        )

    def relay_copy(slot):
        lane = RELAYED.index(slot)
        return pltpu.make_async_remote_copy(
            src_ref=back_s.at[slot], dst_ref=relay_s.at[lane],
            send_sem=back_send.at[slot], recv_sem=relay_recv.at[lane],
            device_id=partner, device_id_type=MESH,
        )

    def onward_copy(slot):
        lane = RELAYED.index(slot)
        return pltpu.make_async_remote_copy(
            src_ref=relay_s.at[lane], dst_ref=back_r.at[slot],
            send_sem=relay_send.at[lane], recv_sem=back_recv.at[slot],
            device_id=following, device_id_type=MESH,
        )

    def send_back(slot):
        if slot not in RELAYED:
            back_copy(slot).start()
            return

        @pl.when(first)
        def _():
            relay_copy(slot).start()

        @pl.when(jnp.logical_not(first))
        def _():
            back_copy(slot).start()

    def pass_on(slot):
        @pl.when(third)
        def _():
            relay_copy(slot).wait_recv()
            onward_copy(slot).start()

    def dq_columns(owner, g):
        return pl.ds(pl.multiple_of(owner * (GROUPS * WIDE) + g * WIDE, WIDE), WIDE)

    def dq_copy(g, i):
        return pltpu.make_async_remote_copy(
            src_ref=dq_s.at[g * TILES + i], dst_ref=dq_ref.at[:, dq_columns(h, g)],
            send_sem=dq_send.at[g * TILES + i], recv_sem=dq_recv.at[g * TILES + h],
            device_id=(s, i), device_id_type=MESH,
        )

    def dq_local(g):
        return pltpu.make_async_copy(
            dq_s.at[g * TILES + h], dq_ref.at[:, dq_columns(h, g)], dq_own.at[g]
        )

    def forward(g, i):
        rows, span = pl.ds(i * TILE, TILE), pl.ds(i * TILE, SPAN)
        keys = k_s[g, span, :]
        bias = bias_s[i]
        for r in range(0, SHARE, PAIR):
            queries = [q_s[g * SHARE + e, rows, :] for e in range(r, r + PAIR)]
            joined = dot(keys, jnp.concatenate(queries, axis=0), NT)
            for e in range(PAIR):
                scores = joined[:, e * HEAD : (e + 1) * HEAD] * SCALE_LOG2 + bias
                top = jnp.max(scores, axis=0, keepdims=True)
                grown = jnp.exp2(scores - top)
                share = 1.0 / jnp.sum(grown, axis=0, keepdims=True)
                prob_s[i, :, pl.ds((r + e) * HEAD, HEAD)] = grown.astype(jnp.bfloat16)
                share_s[i, pl.ds(r + e, 1), :] = share
                column = jnp.broadcast_to(share, (TILE, TILE)).T
                outs = o_s[g * SHARE + r + e, rows, :].astype(jnp.float32) * column
                outs_s[i, pl.ds((r + e) * TILE, TILE), :] = outs.astype(jnp.bfloat16)
        dv_acc[g, span, :] += dot(prob_s[i], outs_s[i], NN)

    def backward(g, i):
        rows, span = pl.ds(i * TILE, TILE), pl.ds(i * TILE, SPAN)
        values = v_s[g, span, :]
        queries = [q_s[g * SHARE + r, rows, :] for r in range(SHARE)]
        rounded = []
        for r in range(0, SHARE, PAIR):
            joined = dot(values, outs_s[i, pl.ds(r * TILE, PAIR * TILE), :], NT)
            for e in range(PAIR):
                grad_probs = joined[:, e * HEAD : (e + 1) * HEAD]
                grown = prob_s[i, :, pl.ds((r + e) * HEAD, HEAD)].astype(jnp.float32)
                delta = jnp.sum(grown * grad_probs, axis=0, keepdims=True)
                delta = delta * share_s[i, pl.ds(r + e, 1), :]
                rounded.append((grown * (grad_probs - delta)).astype(jnp.bfloat16))
        grad_scores = jnp.concatenate(rounded, axis=1)
        dk_acc[g, span, :] += dot(grad_scores, jnp.concatenate(queries, axis=0), NN)
        slot = g * TILES + i
        grads = dot(grad_scores, k_s[g, span, :], TN) * SCALE
        for r in range(SHARE):
            dq_s[slot, :, pl.ds(r * HEAD, HEAD)] = (
                grads[r * HEAD : (r + 1) * HEAD, :].astype(jnp.bfloat16)
            )


    def dq_start(g, i):
        @pl.when(i != h)
        def _():
            dq_copy(g, i).start()

        @pl.when(i == h)
        def _():
            dq_local(g).start()

    def forward_phase(g, parts):
        for part in parts:
            for i in part:
                kv_copy(k_s, 0, g, i).wait()
            for i in part:
                forward(g, i)
        back_s[2 * g] = dv_acc[g, pl.ds(0, BLOCK), :].astype(jnp.bfloat16)
        send_back(2 * g)

    def backward_phase(g, parts):
        for part in parts:
            for i in part:
                kv_copy(v_s, 1, g, i).wait()
            for i in part:
                backward(g, i)
            for i in part:
                dq_start(g, i)
            if part is parts[-1]:
                back_s[2 * g + 1] = (dk_acc[g, pl.ds(0, BLOCK), :] * SCALE).astype(jnp.bfloat16)
                send_back(2 * g + 1)

    for g in range(GROUPS):
        forward_phase(g, PARTS)
        backward_phase(g, PARTS)

    for slot in RELAYED:
        pass_on(slot)

    for g in range(GROUPS):
        columns = pl.ds(g * HEAD, HEAD)
        back_copy(2 * g).wait()
        dv_ref[:, columns] = (
            dv_acc[g, pl.ds(BLOCK, BLOCK), :] + back_r[2 * g].astype(jnp.float32)
        ).astype(jnp.bfloat16)
        back_copy(2 * g + 1).wait()
        dk_ref[:, columns] = (
            dk_acc[g, pl.ds(BLOCK, BLOCK), :] * SCALE + back_r[2 * g + 1].astype(jnp.float32)
        ).astype(jnp.bfloat16)

    for slot in RELAYED:
        @pl.when(third)
        def _(slot=slot):
            onward_copy(slot).wait_send()

    for g in range(GROUPS):
        dq_local(g).wait()
        for i in range(TILES):
            @pl.when(i != h)
            def _(g=g, i=i):
                dq_copy(g, i).wait_send()

        for d in (1, 2, 3):
            owner = lax.rem(h + d, 4)
            pltpu.make_async_remote_copy(
                src_ref=dq_s.at[g * TILES], dst_ref=dq_ref.at[:, dq_columns(owner, g)],
                send_sem=dq_send.at[g * TILES], recv_sem=dq_recv.at[g * TILES + owner],
                device_id=(s, owner), device_id_type=MESH,
            ).wait_recv()


def write_out(a_ref, b_ref, c_ref, a_out, b_out, c_out, sem):
    copies = [
        pltpu.make_async_copy(src, dst, sem.at[slot])
        for slot, (src, dst) in enumerate(((a_ref, a_out), (b_ref, b_out), (c_ref, c_out)))
    ]
    for copy in copies:
        copy.start()
    for copy in copies:
        copy.wait()


def local(n_seq, queries, key_heads, value_head_rows, out_grad, doc_ids):
    bf16, f32 = jnp.bfloat16, jnp.float32
    dma = pltpu.SemaphoreType.DMA
    anywhere = pl.BlockSpec(memory_space=pl.ANY)
    vmem = pl.BlockSpec(memory_space=pltpu.VMEM)
    shapes = (
            jax.ShapeDtypeStruct((TILE, 4 * GROUPS * WIDE), bf16),
            jax.ShapeDtypeStruct((BLOCK, GROUPS * HEAD), bf16),
            jax.ShapeDtypeStruct((BLOCK, GROUPS * HEAD), bf16),
    )
    grads = pl.pallas_call(
        functools.partial(kernel, n_seq),
        out_shape=shapes,
        in_specs=[anywhere] * 5,
        out_specs=(vmem, vmem, vmem),
        scratch_shapes=[
            pltpu.VMEM((GROUPS * SHARE, BLOCK, HEAD), bf16),
            pltpu.VMEM((GROUPS * SHARE, BLOCK, HEAD), bf16),
            pltpu.VMEM((GROUPS, 2 * BLOCK, HEAD), bf16),
            pltpu.VMEM((GROUPS, 2 * BLOCK, HEAD), bf16),
            pltpu.VMEM((TILES, TILE), jnp.int32),
            pltpu.VMEM((TILES, TILE), jnp.int32),
            pltpu.VMEM((2 * TILES, TILE, TILE), f32),
            pltpu.VMEM((TILES, SPAN, TILE), f32),
            pltpu.VMEM((TILES, SPAN, WIDE), bf16),
            pltpu.VMEM((TILES, 8, TILE), f32),
            pltpu.VMEM((TILES, SHARE * TILE, HEAD), bf16),
            pltpu.VMEM((GROUPS, 2 * BLOCK, HEAD), f32),
            pltpu.VMEM((GROUPS, 2 * BLOCK, HEAD), f32),
            pltpu.VMEM((2 * GROUPS, BLOCK, HEAD), bf16),
            pltpu.VMEM((2 * GROUPS, BLOCK, HEAD), bf16),
            pltpu.VMEM((len(RELAYED), BLOCK, HEAD), bf16),
            pltpu.VMEM((GROUPS * TILES, TILE, WIDE), bf16),
            dma((1 + 2 * GROUPS + 2 * GROUPS * SHARE,)),
            dma((2 * GROUPS * TILES,)),
            dma((2 * GROUPS * TILES,)),
            dma(()),
            dma(()),
            dma((GROUPS * TILES,)),
            dma((GROUPS * TILES,)),
            dma((GROUPS,)),
            dma((2 * GROUPS,)),
            dma((2 * GROUPS,)),
            dma((len(RELAYED),)),
            dma((len(RELAYED),)),
        ],
        compiler_params=pltpu.CompilerParams(
            collective_id=0, has_side_effects=True, vmem_limit_bytes=48 * 2**20
        ),
    )(*[pltpu.with_memory_space_constraint(a, pltpu.HBM) for a in (queries, key_heads, value_head_rows, out_grad, doc_ids.reshape(TILES, TILE))])

    return pl.pallas_call(
        write_out,
        out_shape=shapes,
        in_specs=[vmem] * 3,
        out_specs=(anywhere,) * 3,
        scratch_shapes=[dma((3,))],
    )(*[pltpu.with_memory_space_constraint(a, pltpu.VMEM) for a in grads])


def solution(mesh):
    placed = (P("seq", "head"), P("seq", "head"), P("seq", "head"), P("seq", "head"), P("seq"))
    return jax.shard_map(
        functools.partial(local, mesh.shape["seq"]),
        mesh=mesh,
        in_specs=placed,
        out_specs=(P(("seq", "head"), None), P("seq", "head"), P("seq", "head")),
        check_vma=False,
    )
```
